32 devices in a mesh: group: 1, row: 32 (over z, y, x, core), col: 1.
Axes of the slice: x: 2, y: 2, z: 4, core: 2. Of those that a mesh axis runs over, the one named last changes fastest.
Arguments:
- field: bfloat16 [1280, 32, 8192], P(('group', 'row'), None, 'col'), may hold values from -6 to 6
- spec_weight: bfloat16 [2, 128, 32, 32, 128], P(None, 'row', None, None, 'col'), may hold values from -0.75 to 0.75
- point_weight: bfloat16 [32, 32], replicated, may hold values from -1 to 1
- bias: float32 [32], replicated, may hold values from -3 to 3
Outputs:
- output: bfloat16 [1280, 32, 8192], P(('group', 'row'), None, 'col')
The draws below stay inside these ranges and needn't reach their ends.
All inputs are finite; a program needn't handle non-finite values.
Results may differ from the reference program's by a relative error of at most 0.0059.
Values may be sent and summed in bfloat16 or wider, within the bound.
A program may use at most 128 MiB of HBM per device.

```python
import math
import jax
import jax.numpy as jnp
from jax import lax

C = 32
NY = 8192
KX = 128
KY = 128
NX = 1280


def block_scale(rng, dims, shards, least, high):
    gain = 1.0
    for axis_at, parts in shards:
        draws = jax.random.uniform(jax.random.fold_in(jax.random.fold_in(rng, 6), axis_at), (parts,), jnp.float32, least / len(shards), high / len(shards))
        gain = gain * jnp.repeat(jnp.exp(draws), dims[axis_at] // parts).reshape((-1,) + (1,) * (len(dims) - 1 - axis_at))
    return gain


def normal_values(key, shape, scale, reach, shards=(), held_as=jnp.bfloat16):
    entries = jax.random.normal(key, shape, jnp.float32) * scale
    if len(shards) > 0:
        entries = block_scale(key, shape, shards, -0.22, 0.18) * entries
    return jnp.clip(entries, min=-reach, max=reach).astype(held_as)


def setup_inputs(seed: int = 0, part: int = 0) -> dict:
    key_of = jax.random.split(jax.random.key(seed), 5)
    own_keys = jax.random.split(jax.random.fold_in(key_of[4], part), 5)
    return {
        "field": normal_values(own_keys[0], (NX, C, NY), 1.0, 6.0, ((0, 32),)),
        "spec_weight": normal_values(key_of[1], (2, KX, C, C, KY), (2 * C) ** -0.5, 0.75, ((1, 32),)),
        "point_weight": normal_values(key_of[2], (C, C), C ** -0.5, 1.0),
        "bias": normal_values(key_of[3], (C,), 0.5, 3.0, (), jnp.float32),
    }


def forward_columns(y_global, modes_y, length_y):
    freq = jnp.arange(modes_y, dtype=jnp.int32)
    phase = (y_global[:, None] * freq[None, :] % length_y).astype(jnp.float32) * (2.0 * math.pi / length_y)
    scale = 1.0 / math.sqrt(length_y)
    return jnp.concatenate([jnp.cos(phase) * scale, -jnp.sin(phase) * scale], axis=1).astype(jnp.bfloat16)

def row_phase(x_global, modes_x, length_x):
    index = jnp.arange(modes_x, dtype=jnp.int32)
    freq = jnp.where(index < modes_x // 2, index, index - modes_x + length_x).astype(jnp.int32)
    return (freq[:, None] * x_global[None, :] % length_x).astype(jnp.float32) * (2.0 * math.pi / length_x)

def forward_rows(x_global, modes_x, length_x):
    phase = row_phase(x_global, modes_x, length_x)
    scale = 1.0 / math.sqrt(length_x)
    return (jnp.cos(phase) * scale, jnp.sin(phase) * scale)

def inverse_row_tables(x_global, modes_x, length_x):
    phase = row_phase(x_global, modes_x, length_x).T
    return (jnp.cos(phase).astype(jnp.bfloat16), jnp.sin(phase).astype(jnp.bfloat16))

def inverse_columns(y_global, modes_y, modes_x):
    freq = jnp.arange(modes_y, dtype=jnp.int32)
    phase = (freq[:, None] * y_global[None, :] % NY).astype(jnp.float32) * (2.0 * math.pi / NY)
    factor = jnp.where(freq == 0, 1.0, 2.0).astype(jnp.float32)[:, None] / math.sqrt(2.0 * modes_x * modes_y)
    return jnp.concatenate([factor * jnp.cos(phase), -factor * jnp.sin(phase)], axis=0).astype(jnp.bfloat16)

def row_section(partial_value, cosine, sine):
    highest = lax.Precision.HIGHEST
    real_part = partial_value[:, :, 0]
    imag_part = partial_value[:, :, 1]
    out_real = jnp.einsum('jx,xck->jck', cosine, real_part, precision=highest) + jnp.einsum('jx,xck->jck', sine, imag_part, precision=highest)
    out_imag = jnp.einsum('jx,xck->jck', cosine, imag_part, precision=highest) - jnp.einsum('jx,xck->jck', sine, real_part, precision=highest)
    return jnp.stack([out_real, out_imag])

def mix_modes(spectrum, spec_weight):
    weights = spec_weight.astype(jnp.float32)
    highest = lax.Precision.HIGHEST
    spec_real = spectrum[0]
    spec_imag = spectrum[1]
    out_real = jnp.einsum('jik,jiok->jok', spec_real, weights[0], precision=highest) - jnp.einsum('jik,jiok->jok', spec_imag, weights[1], precision=highest)
    out_imag = jnp.einsum('jik,jiok->jok', spec_real, weights[1], precision=highest) + jnp.einsum('jik,jiok->jok', spec_imag, weights[0], precision=highest)
    return jnp.stack([out_real, out_imag]).astype(jnp.bfloat16)

def reference(field, spec_weight, point_weight, bias):
    x_global = jnp.arange(NX, dtype=jnp.int32)
    y_global = jnp.arange(NY, dtype=jnp.int32)
    table_y = forward_columns(y_global, KY, NY)
    partial_value = jnp.dot(field.reshape(NX * C, NY), table_y, preferred_element_type=jnp.float32).reshape(NX, C, 2, KY)
    cosine, sine = forward_rows(x_global, KX, NX)
    spectrum = row_section(partial_value, cosine, sine)
    mixed = mix_modes(spectrum, spec_weight)
    inv_cos, inv_sin = inverse_row_tables(x_global, KX, NX)
    inv_cos = inv_cos.astype(jnp.float32)
    inv_sin = inv_sin.astype(jnp.float32)
    mixed_real = mixed[0].astype(jnp.float32)
    mixed_imag = mixed[1].astype(jnp.float32)
    half_real = jnp.einsum('xj,jok->xok', inv_cos, mixed_real) - jnp.einsum('xj,jok->xok', inv_sin, mixed_imag)
    half_imag = jnp.einsum('xj,jok->xok', inv_sin, mixed_real) + jnp.einsum('xj,jok->xok', inv_cos, mixed_imag)
    inverse_half = jnp.stack([half_real, half_imag], axis=2).astype(jnp.bfloat16)
    table_back = inverse_columns(y_global, KY, KX)
    spectral = jnp.dot(inverse_half.reshape(NX * C, 2 * KY), table_back, preferred_element_type=jnp.float32).reshape(NX, C, NY)
    pointwise = jnp.einsum('oi,xiy->xoy', point_weight.astype(jnp.float32), field.astype(jnp.float32))
    total = spectral + pointwise + bias[None, :, None]
    return jax.nn.gelu(total, approximate=True).astype(jnp.bfloat16)
```

```python
import functools
import math

import jax
import jax.numpy as jnp
import ml_dtypes
import numpy as np
from jax import lax
from jax.experimental import pallas as pl
from jax.experimental.pallas import tpu as pltpu
from jax.sharding import PartitionSpec as P

BF16 = ml_dtypes.bfloat16
MESH = pl.DeviceIdType.MESH
REMOTE = True


def phases(first, second, length):
    index = (first[:, None].astype(np.int64) * second[None, :]) % length
    return index.astype(np.float32) * np.float32(2.0 * math.pi / length)


def column_tables(modes_x, modes_y, length_y):
    freq = np.arange(modes_y)
    phase = phases(np.arange(length_y), freq, length_y)
    cosine, sine = np.cos(phase), np.sin(phase)
    scale = np.float32(1.0 / math.sqrt(length_y))
    forward = np.concatenate([cosine * scale, -sine * scale], axis=1).astype(BF16)
    factor = np.where(freq == 0, 1.0, 2.0).astype(np.float32) / np.float32(
        math.sqrt(2.0 * modes_x * modes_y)
    )
    inverse = np.concatenate([factor * cosine, -factor * sine], axis=1).T.astype(BF16)
    return forward, np.ascontiguousarray(inverse)


def row_tables(row_devices, block_x, row_count):
    modes_x, length_x = row_devices * block_x, row_devices * row_count
    index = np.arange(modes_x)
    freq = np.where(index < modes_x // 2, index, index - modes_x + length_x)
    phase = phases(freq, np.arange(length_x), length_x)
    shape = (row_devices, 1, block_x, row_devices, 1, row_count)
    cosine, sine = np.cos(phase).reshape(shape), np.sin(phase).reshape(shape)
    table = np.concatenate(
        [np.concatenate([cosine, sine], axis=4), np.concatenate([-sine, cosine], axis=4)], axis=1
    ).reshape(2 * modes_x, 2 * length_x)
    scaled = table * np.float32(1.0 / math.sqrt(length_x))
    high = scaled.astype(BF16)
    low = (scaled - high.astype(np.float32)).astype(BF16)
    return high, low, np.ascontiguousarray(table.T).astype(BF16)


def regroup(rows, channels):
    out = np.zeros((rows * channels, rows * channels), BF16)
    for row in range(rows):
        for channel in range(channels):
            out[channel * rows + row, row * channels + channel] = 1
    return out


CHUNK = 8


def forward_kernel(steps, field_ref, table_ref, perm_ref, out_ref, total, ordered):
    step = pl.program_id(0)
    rows, channels, width = field_ref.shape
    modes = out_ref.shape[2]

    @pl.when(step == 0)
    def _():
        total[...] = jnp.zeros_like(total)

    total[...] += jnp.dot(
        field_ref[...].reshape(rows * channels, width),
        table_ref[...],
        preferred_element_type=jnp.float32,
    )

    @pl.when(step == steps - 1)
    def _():
        size = CHUNK * channels
        for chunk in range(rows // CHUNK):
            part = total[chunk * size : (chunk + 1) * size, :]
            if out_ref.dtype == jnp.float32:
                moved = jnp.dot(
                    perm_ref[...].astype(jnp.float32),
                    part,
                    preferred_element_type=jnp.float32,
                    precision=lax.Precision.HIGHEST,
                )
            else:
                moved = jnp.dot(
                    perm_ref[...], part.astype(jnp.bfloat16), preferred_element_type=jnp.float32
                )
            moved = moved.reshape(channels, CHUNK, 2 * modes)
            at = chunk * CHUNK
            ordered[:, at : at + CHUNK, :] = moved[:, :, :modes]
            ordered[:, rows + at : rows + at + CHUNK, :] = moved[:, :, modes:]
        out_ref[...] = ordered[...].astype(out_ref.dtype)


def forward(field, table, out_type):
    rows, channels, cols = field.shape
    modes = table.shape[1] // 2
    width = min(cols, 1024)
    steps = cols // width
    perm = regroup(CHUNK, channels)
    return pl.pallas_call(
        functools.partial(forward_kernel, steps),
        out_shape=jax.ShapeDtypeStruct((channels, 2 * rows, modes), out_type),
        grid=(steps,),
        in_specs=[
            pl.BlockSpec((rows, channels, width), lambda y: (0, 0, y)),
            pl.BlockSpec((width, 2 * modes), lambda y: (y, 0)),
            pl.BlockSpec(perm.shape, lambda y: (0, 0)),
        ],
        out_specs=pl.BlockSpec((channels, 2 * rows, modes), lambda y: (0, 0, 0)),
        scratch_shapes=[
            pltpu.VMEM((rows * channels, 2 * modes), jnp.float32),
            pltpu.VMEM((channels, 2 * rows, modes), jnp.float32),
        ],
        compiler_params=pltpu.CompilerParams(vmem_limit_bytes=40 * 1024 * 1024),
        cost_estimate=pl.CostEstimate(
            flops=2 * rows * channels * cols * 2 * modes,
            bytes_accessed=2 * (rows * channels * cols + cols * 2 * modes),
            transcendentals=0,
        ),
    )(field, table, jnp.asarray(perm))


def inverse_kernel(field_ref, half_ref, table_ref, point_ref, bias_ref, out_ref):
    rows, channels, width = field_ref.shape
    size = CHUNK * channels
    tile = min(width, 256)

    @pl.loop(0, rows // CHUNK)
    def _(chunk):
        at = pl.multiple_of(chunk * CHUNK, CHUNK)
        half = half_ref[pl.ds(at, CHUNK)].reshape(size, half_ref.shape[2])
        for col in range(0, width, tile):
            values = field_ref[pl.ds(at, CHUNK), :, col : col + tile].reshape(size, tile)
            x = (
                jnp.dot(half, table_ref[:, col : col + tile], preferred_element_type=jnp.float32)
                + jnp.dot(point_ref[...], values, preferred_element_type=jnp.float32)
                + bias_ref[:, :tile]
            )
            inner = x * (math.sqrt(2.0 / math.pi) * 0.044715 * (x * x) + math.sqrt(2.0 / math.pi))
            scaled = 0.5 * x
            y = scaled * jnp.tanh(inner) + scaled
            out_ref[pl.ds(at, CHUNK), :, col : col + tile] = y.astype(out_ref.dtype).reshape(
                CHUNK, channels, tile
            )


def inverse(field, half, table, point_weight, bias):
    rows, channels, cols = field.shape
    depth = table.shape[0]
    width = min(cols, 1024)
    size = CHUNK * channels
    point = jnp.kron(jnp.eye(CHUNK, dtype=point_weight.dtype), point_weight)
    spread = jnp.broadcast_to(jnp.tile(bias, CHUNK)[:, None], (size, min(width, 256)))
    return pl.pallas_call(
        inverse_kernel,
        out_shape=jax.ShapeDtypeStruct(field.shape, jnp.bfloat16),
        grid=(cols // width,),
        in_specs=[
            pl.BlockSpec((rows, channels, width), lambda y: (0, 0, y)),
            pl.BlockSpec((rows, channels, depth), lambda y: (0, 0, 0)),
            pl.BlockSpec((depth, width), lambda y: (0, y)),
            pl.BlockSpec(point.shape, lambda y: (0, 0)),
            pl.BlockSpec(spread.shape, lambda y: (0, 0)),
        ],
        out_specs=pl.BlockSpec((rows, channels, width), lambda y: (0, 0, y)),
        compiler_params=pltpu.CompilerParams(vmem_limit_bytes=40 * 1024 * 1024),
        cost_estimate=pl.CostEstimate(
            flops=2 * rows * channels * cols * (depth + size),
            bytes_accessed=4 * rows * channels * cols,
            transcendentals=rows * channels * cols,
        ),
    )(field, half, table, point, spread)


def mix_modes(spectrum, spec_weight):
    weights = spec_weight.astype(jnp.float32)
    real, imag = spectrum[:, 0], spectrum[:, 1]
    product = functools.partial(jnp.einsum, "ijk,jiok->ojk", precision=lax.Precision.HIGHEST)
    out_real = product(real, weights[0]) - product(imag, weights[1])
    out_imag = product(real, weights[1]) + product(imag, weights[0])
    return jnp.stack([out_real, out_imag], axis=1).astype(jnp.bfloat16)


def swap(blocks):
    count, own, rows, modes = blocks.shape
    got = lax.all_to_all(blocks, "row", 0, 0, tiled=True)
    return got.transpose(1, 0, 2, 3).reshape(own, count * rows, modes)


def give(values, count):
    own, size, modes = values.shape
    blocks = values.reshape(own, count, size // count, modes).transpose(1, 0, 2, 3)
    got = lax.all_to_all(blocks, "row", 0, 0, tiled=True)
    return got.reshape(count * own, size // count, modes)


def middle(partial_value, spec_weight, tables):
    high, low, back = tables
    channels, rows, modes = partial_value.shape
    count = lax.axis_size("row")
    block_x = spec_weight.shape[1]
    part = swap(partial_value.reshape(count, channels // count, rows, modes))
    transform = functools.partial(
        jnp.einsum, "am,cmk->cak", preferred_element_type=jnp.float32
    )
    spectrum = give(transform(high, part) + transform(low, part), count)
    mixed = mix_modes(spectrum.reshape(channels, 2, block_x, modes), spec_weight)
    mixed = swap(mixed.reshape(count, channels // count, 2 * block_x, modes))
    half = jnp.einsum("ma,cak->cmk", back, mixed, preferred_element_type=jnp.float32)
    return give(half.astype(jnp.bfloat16), count)


def middle_kernel(
    n, part_ref, high_hbm, low_hbm, back_hbm, weight_hbm, out_ref,
    high, low, back, weight, part_in, spec_out, spec_in, mix_out, mix_in, half_out,
    load_sem, send_sem, recv_sem,
):
    me = lax.axis_index("row")
    block_x, channels = weight.shape[1], weight.shape[3]
    modes = weight.shape[4]
    pairs = [(high_hbm, high), (low_hbm, low), (weight_hbm, weight), (back_hbm, back)]
    loads = [
        pltpu.make_async_copy(src, dst, load_sem.at[at]) for at, (src, dst) in enumerate(pairs)
    ]
    for load in loads:
        load.start()

    barrier = pltpu.get_barrier_semaphore()

    @pl.loop(1, n)
    def _(shift):
        pl.semaphore_signal(
            barrier, inc=1, device_id={"row": lax.rem(me + shift, n)}, device_id_type=MESH
        )

    pl.semaphore_wait(barrier, n - 1)

    def copy(phase, src, dst, shift):
        to = lax.rem(me + shift, n)
        return pltpu.make_async_remote_copy(
            src_ref=src.at[to],
            dst_ref=dst.at[me],
            send_sem=send_sem.at[phase, shift],
            recv_sem=recv_sem.at[phase, shift],
            device_id={"row": to},
            device_id_type=MESH,
        )

    def exchange(phase, src, dst):
        @pl.loop(1, n)
        def _(shift):
            copy(phase, src, dst, shift).start()

        dst[me] = src[me]

        @pl.loop(1, n)
        def _(shift):
            copy(phase, src, dst, shift).wait_recv()

    exchange(0, part_ref, part_in)
    loads[0].wait()
    loads[1].wait()
    part = part_in[...].reshape(n * part_in.shape[1], modes)
    spectrum = jnp.dot(high[...], part, preferred_element_type=jnp.float32) + jnp.dot(
        low[...], part, preferred_element_type=jnp.float32
    )
    spec_out[...] = spectrum.reshape(spec_out.shape)
    exchange(1, spec_out, spec_in)
    loads[2].wait()
    for mode in range(block_x):

        def add(at, sums, mode=mode):
            real, imag = sums
            a = spec_in[at, mode : mode + 1, :]
            b = spec_in[at, block_x + mode : block_x + mode + 1, :]
            c = weight[0, mode, at].astype(jnp.float32)
            d = weight[1, mode, at].astype(jnp.float32)
            return real + (a * c - b * d), imag + (a * d + b * c)

        zero = jnp.zeros((channels, modes), jnp.float32)
        real, imag = lax.fori_loop(0, channels, add, (zero, zero))
        mix_out[:, mode, :] = real
        mix_out[:, block_x + mode, :] = imag
    exchange(2, mix_out, mix_in)
    loads[3].wait()
    mixed = mix_in[...].reshape(n * 2 * block_x, modes).astype(jnp.bfloat16)
    half = jnp.dot(back[...], mixed, preferred_element_type=jnp.float32)
    half_out[...] = half.astype(jnp.bfloat16).reshape(half_out.shape)
    exchange(3, half_out, out_ref)
    for phase, (src, dst) in enumerate(
        [(part_ref, part_in), (spec_out, spec_in), (mix_out, mix_in), (half_out, out_ref)]
    ):

        @pl.loop(1, n)
        def _(shift, phase=phase, src=src, dst=dst):
            copy(phase, src, dst, shift).wait_send()


def remote_middle(partial_value, spec_weight, tables):
    count = lax.axis_size("row")
    channels, rows, modes = partial_value.shape
    block_x = spec_weight.shape[1]
    vmem = pl.BlockSpec(memory_space=pltpu.VMEM)
    wide = pltpu.VMEM(partial_value.shape, jnp.bfloat16)
    narrow = pltpu.VMEM((channels, 2 * block_x, modes), jnp.float32)
    return pl.pallas_call(
        functools.partial(middle_kernel, count),
        out_shape=jax.ShapeDtypeStruct(partial_value.shape, jnp.bfloat16),
        in_specs=[vmem] + [pl.BlockSpec(memory_space=pl.ANY)] * 4,
        out_specs=vmem,
        scratch_shapes=[pltpu.VMEM(table.shape, jnp.bfloat16) for table in tables]
        + [pltpu.VMEM(spec_weight.shape, jnp.bfloat16)]
        + [wide, narrow, narrow, narrow, narrow, wide]
        + [
            pltpu.SemaphoreType.DMA((4,)),
            pltpu.SemaphoreType.DMA((4, count)),
            pltpu.SemaphoreType.DMA((4, count)),
        ],
        compiler_params=pltpu.CompilerParams(
            collective_id=0, has_side_effects=True, vmem_limit_bytes=32 * 1024 * 1024
        ),
    )(partial_value, *tables, spec_weight)


def shards(field, spec_weight, point_weight, bias):
    row_count, chan_count, col_count = field.shape
    row_devices = lax.axis_size("row")
    col_devices = lax.axis_size("col")
    block_x = spec_weight.shape[1]
    modes_y = spec_weight.shape[4] * col_devices
    modes_x = block_x * row_devices
    table_y, table_back = column_tables(modes_x, modes_y, col_count * col_devices)
    table_y, table_back = jnp.asarray(table_y), jnp.asarray(table_back)
    tables = [jnp.asarray(table) for table in row_tables(row_devices, block_x, row_count)]
    if col_devices > 1:
        start = lax.axis_index("col") * col_count
        table_y = lax.dynamic_slice_in_dim(table_y, start, col_count, 0)
        table_back = lax.dynamic_slice_in_dim(table_back, start, col_count, 1)
        whole = forward(field, table_y, jnp.float32)
        own = lax.psum_scatter(whole, "col", scatter_dimension=2, tiled=True)
        half = middle(own.astype(jnp.bfloat16), spec_weight, tables)
        half = lax.all_gather(half, "col", axis=2, tiled=True)
    else:
        partial_value = forward(field, table_y, jnp.bfloat16)
        if REMOTE and chan_count == row_devices:
            half = remote_middle(partial_value, spec_weight, tables)
        else:
            half = middle(partial_value, spec_weight, tables)
    half = half.reshape(chan_count, 2, row_count, modes_y).transpose(2, 0, 1, 3)
    half = half.reshape(row_count, chan_count, 2 * modes_y)
    return inverse(field, half, table_back, point_weight, bias)


def solution(mesh):
    placed = (P(("group", "row"), None, "col"), P(None, "row", None, None, "col"), P(), P())
    return jax.shard_map(
        shards,
        mesh=mesh,
        in_specs=placed,
        out_specs=P(("group", "row"), None, "col"),
        check_vma=False,
    )
```

```python
import functools
import math

import jax
import jax.numpy as jnp
import ml_dtypes
import numpy as np
from jax import lax
from jax.experimental import pallas as pl
from jax.experimental.pallas import tpu as pltpu
from jax.sharding import PartitionSpec as P

BF16 = ml_dtypes.bfloat16
MESH = pl.DeviceIdType.MESH


def phases(first, second, length):
    index = (first[:, None].astype(np.int64) * second[None, :]) % length
    return index.astype(np.float32) * np.float32(2.0 * math.pi / length)


def column_tables(modes_x, modes_y, length_y):
    freq = np.arange(modes_y)
    phase = phases(np.arange(length_y), freq, length_y)
    cosine, sine = np.cos(phase), np.sin(phase)
    scale = np.float32(1.0 / math.sqrt(length_y))
    forward = np.concatenate([cosine * scale, -sine * scale], axis=1).astype(BF16)
    factor = np.where(freq == 0, 1.0, 2.0).astype(np.float32) / np.float32(
        math.sqrt(2.0 * modes_x * modes_y)
    )
    inverse = np.concatenate([factor * cosine, -factor * sine], axis=1).T.astype(BF16)
    halved = (0.5 * inverse.astype(np.float32)).astype(BF16)
    return forward, np.ascontiguousarray(halved)


def row_tables(row_devices, block_x, row_count):
    modes_x, length_x = row_devices * block_x, row_devices * row_count
    index = np.arange(modes_x)
    freq = np.where(index < modes_x // 2, index, index - modes_x + length_x)
    phase = phases(freq, np.arange(length_x), length_x)
    shape = (row_devices, 1, block_x, row_devices, 1, row_count)
    cosine, sine = np.cos(phase).reshape(shape), np.sin(phase).reshape(shape)
    table = np.concatenate(
        [np.concatenate([cosine, sine], axis=4), np.concatenate([-sine, cosine], axis=4)], axis=1
    ).reshape(2 * modes_x, 2 * length_x)
    scaled = table * np.float32(1.0 / math.sqrt(length_x))
    high = scaled.astype(BF16)
    low = (scaled - high.astype(np.float32)).astype(BF16)
    return high, low, np.ascontiguousarray(table.T).astype(BF16)


def regroup(rows, channels):
    out = np.zeros((rows * channels, rows * channels), BF16)
    for row in range(rows):
        for channel in range(channels):
            out[channel * rows + row, row * channels + channel] = 1
    return out


CHUNK = 8


def forward_kernel(steps, field_ref, table_ref, perm_ref, out_ref, total, ordered):
    step = pl.program_id(0)
    rows, channels, width = field_ref.shape
    modes = out_ref.shape[2]

    @pl.when(step == 0)
    def _():
        total[...] = jnp.zeros_like(total)

    total[...] += jnp.dot(
        field_ref[...].reshape(rows * channels, width),
        table_ref[...],
        preferred_element_type=jnp.float32,
    )

    @pl.when(step == steps - 1)
    def _():
        size = CHUNK * channels
        for chunk in range(rows // CHUNK):
            part = total[chunk * size : (chunk + 1) * size, :]
            if out_ref.dtype == jnp.float32:
                moved = jnp.dot(
                    perm_ref[...].astype(jnp.float32),
                    part,
                    preferred_element_type=jnp.float32,
                    precision=lax.Precision.HIGHEST,
                )
            else:
                moved = jnp.dot(
                    perm_ref[...], part.astype(jnp.bfloat16), preferred_element_type=jnp.float32
                )
            moved = moved.reshape(channels, CHUNK, 2 * modes)
            at = chunk * CHUNK
            ordered[:, at : at + CHUNK, :] = moved[:, :, :modes]
            ordered[:, rows + at : rows + at + CHUNK, :] = moved[:, :, modes:]
        out_ref[...] = ordered[...].astype(out_ref.dtype)


def forward(field, table, out_type):
    rows, channels, cols = field.shape
    modes = table.shape[1] // 2
    width = min(cols, 2048)
    steps = cols // width
    perm = regroup(CHUNK, channels)
    return pl.pallas_call(
        functools.partial(forward_kernel, steps),
        out_shape=jax.ShapeDtypeStruct((channels, 2 * rows, modes), out_type),
        grid=(steps,),
        in_specs=[
            pl.BlockSpec((rows, channels, width), lambda y: (0, 0, y)),
            pl.BlockSpec((width, 2 * modes), lambda y: (y, 0)),
            pl.BlockSpec(perm.shape, lambda y: (0, 0)),
        ],
        out_specs=pl.BlockSpec((channels, 2 * rows, modes), lambda y: (0, 0, 0)),
        scratch_shapes=[
            pltpu.VMEM((rows * channels, 2 * modes), jnp.float32),
            pltpu.VMEM((channels, 2 * rows, modes), jnp.float32),
        ],
        compiler_params=pltpu.CompilerParams(vmem_limit_bytes=60 * 1024 * 1024),
        cost_estimate=pl.CostEstimate(
            flops=2 * rows * channels * cols * 2 * modes,
            bytes_accessed=2 * (rows * channels * cols + cols * 2 * modes),
            transcendentals=0,
        ),
    )(field, table, jnp.asarray(perm))


def inverse_kernel(field_ref, half_ref, table_ref, point_ref, bias_ref, out_ref):
    rows, channels, width = field_ref.shape
    size = CHUNK * channels
    tile = min(width, 256)

    @pl.loop(0, rows // CHUNK)
    def _(chunk):
        at = pl.multiple_of(chunk * CHUNK, CHUNK)
        half = half_ref[pl.ds(at, CHUNK)].reshape(size, half_ref.shape[2])
        for col in range(0, width, tile):
            values = field_ref[pl.ds(at, CHUNK), :, col : col + tile].reshape(size, tile)
            x = (
                jnp.dot(half, table_ref[:, col : col + tile], preferred_element_type=jnp.float32)
                + jnp.dot(point_ref[...], values, preferred_element_type=jnp.float32)
                + bias_ref[:, :tile]
            )
            rate = 2.0 * math.sqrt(2.0 / math.pi)
            y = x * jnp.tanh(x * (rate * 4.0 * 0.044715 * (x * x) + rate)) + x
            out_ref[pl.ds(at, CHUNK), :, col : col + tile] = y.astype(out_ref.dtype).reshape(
                CHUNK, channels, tile
            )


def inverse(field, half, table, point, spread):
    rows, channels, cols = field.shape
    depth = table.shape[0]
    width = min(cols, 2048)
    size = CHUNK * channels
    return pl.pallas_call(
        inverse_kernel,
        out_shape=jax.ShapeDtypeStruct(field.shape, jnp.bfloat16),
        grid=(cols // width,),
        in_specs=[
            pl.BlockSpec((rows, channels, width), lambda y: (0, 0, y)),
            pl.BlockSpec((rows, channels, depth), lambda y: (0, 0, 0)),
            pl.BlockSpec((depth, width), lambda y: (0, y)),
            pl.BlockSpec(point.shape, lambda y: (0, 0)),
            pl.BlockSpec(spread.shape, lambda y: (0, 0)),
        ],
        out_specs=pl.BlockSpec((rows, channels, width), lambda y: (0, 0, y)),
        compiler_params=pltpu.CompilerParams(vmem_limit_bytes=60 * 1024 * 1024),
        cost_estimate=pl.CostEstimate(
            flops=2 * rows * channels * cols * (depth + size),
            bytes_accessed=4 * rows * channels * cols,
            transcendentals=rows * channels * cols,
        ),
    )(field, half, table, point, spread)


def mix_modes(spectrum, spec_weight):
    weights = spec_weight.astype(jnp.float32)
    real, imag = spectrum[:, 0], spectrum[:, 1]
    product = functools.partial(jnp.einsum, "ijk,jiok->ojk", precision=lax.Precision.HIGHEST)
    out_real = product(real, weights[0]) - product(imag, weights[1])
    out_imag = product(real, weights[1]) + product(imag, weights[0])
    return jnp.stack([out_real, out_imag], axis=1).astype(jnp.bfloat16)


def swap(blocks):
    count, own, rows, modes = blocks.shape
    got = lax.all_to_all(blocks, "row", 0, 0, tiled=True)
    return got.transpose(1, 0, 2, 3).reshape(own, count * rows, modes)


def give(values, count):
    own, size, modes = values.shape
    blocks = values.reshape(own, count, size // count, modes).transpose(1, 0, 2, 3)
    got = lax.all_to_all(blocks, "row", 0, 0, tiled=True)
    return got.reshape(count * own, size // count, modes)


def middle(partial_value, spec_weight, tables):
    high, low, back = tables
    channels, rows, modes = partial_value.shape
    count = lax.axis_size("row")
    block_x = spec_weight.shape[1]
    part = swap(partial_value.reshape(count, channels // count, rows, modes))
    transform = functools.partial(
        jnp.einsum, "am,cmk->cak", preferred_element_type=jnp.float32
    )
    spectrum = give(transform(high, part) + transform(low, part), count)
    mixed = mix_modes(spectrum.reshape(channels, 2, block_x, modes), spec_weight)
    mixed = swap(mixed.reshape(count, channels // count, 2 * block_x, modes))
    half = jnp.einsum("ma,cak->cmk", back, mixed, preferred_element_type=jnp.float32)
    return give(half.astype(jnp.bfloat16), count)


PLANE = 8


def middle_kernel(
    outer, part_ref, point_ref, bias_ref, high_hbm, low_hbm, back_hbm, weight_hbm,
    out_ref, point_out, bias_out,
    high, low, back, weight, part_in, sums, partial_out, partial_in, spec_out, spec_in,
    mix_out, mix_in, modes_in, half_out, load_sem, send_sem, recv_sem,
):
    me = lax.axis_index("row")
    level, place = me // PLANE, lax.rem(me, PLANE)
    block_x, channels, modes = weight.shape[1], weight.shape[3], weight.shape[4]
    own = channels // PLANE
    span = high.shape[1]
    start = pl.multiple_of(level * span, span)
    pairs = [
        (high_hbm.at[:, pl.ds(start, span)], high),
        (low_hbm.at[:, pl.ds(start, span)], low),
        (weight_hbm, weight),
        (back_hbm.at[pl.ds(start, span), :], back),
    ]
    loads = [
        pltpu.make_async_copy(src, dst, load_sem.at[at]) for at, (src, dst) in enumerate(pairs)
    ]
    for load in loads:
        load.start()

    def in_plane(shift):
        return lax.rem(place + shift, PLANE)

    def in_line(shift):
        return lax.rem(level + shift, outer)

    barrier = pltpu.get_barrier_semaphore()

    @pl.loop(1, PLANE)
    def _(shift):
        to = level * PLANE + in_plane(shift)
        pl.semaphore_signal(barrier, inc=1, device_id={"row": to}, device_id_type=MESH)

    @pl.loop(1, outer)
    def _(shift):
        to = in_line(shift) * PLANE + place
        pl.semaphore_signal(barrier, inc=1, device_id={"row": to}, device_id_type=MESH)

    size = bias_out.shape[0]
    shape = (size, channels)
    pick = lax.broadcasted_iota(jnp.int32, shape, 0) % channels == lax.broadcasted_iota(
        jnp.int32, shape, 1
    )
    pick = pick.astype(jnp.float32)
    along = (((1,), (1,)), ((), ()))
    tall = jnp.dot(pick.astype(jnp.bfloat16), point_ref[...], preferred_element_type=jnp.float32)
    full = lax.dot_general(
        tall.astype(jnp.bfloat16),
        pick.astype(jnp.bfloat16),
        along,
        preferred_element_type=jnp.float32,
    )
    shape = (size, size)
    same = lax.broadcasted_iota(jnp.int32, shape, 0) // channels == lax.broadcasted_iota(
        jnp.int32, shape, 1
    ) // channels
    point_out[...] = jnp.where(same, 0.5 * full, 0.0).astype(jnp.bfloat16)
    bias_out[...] = 0.5 * lax.dot_general(
        pick,
        jnp.broadcast_to(bias_ref[...], (size, channels)),
        along,
        preferred_element_type=jnp.float32,
        precision=lax.Precision.HIGHEST,
    )
    pl.semaphore_wait(barrier, PLANE - 1 + outer - 1)

    def copy(src, dst, phase, piece, shift, to):
        return pltpu.make_async_remote_copy(
            src_ref=src,
            dst_ref=dst,
            send_sem=send_sem.at[phase, piece, shift],
            recv_sem=recv_sem.at[phase, piece, shift],
            device_id={"row": to},
            device_id_type=MESH,
        )

    def plane_copy(phase, piece, shift):
        to = in_plane(shift)
        src, dst = [
            lambda: (part_ref.at[to * own + piece], part_in.at[piece, place]),
            lambda: (spec_out.at[to], spec_in.at[place]),
            lambda: (mix_out.at[to], mix_in.at[place]),
            lambda: (half_out.at[piece, to], out_ref.at[place * own + piece]),
        ][phase]()
        return copy(src, dst, phase, piece, shift, level * PLANE + to)

    def line_copy(phase, piece, shift):
        to = in_line(shift)
        src, dst = [
            lambda: (partial_out.at[piece, to], partial_in.at[piece, shift]),
            lambda: (modes_in.at[piece, level], modes_in.at[piece, level]),
        ][phase]()
        return copy(src, dst, 4 + phase, piece, shift, to * PLANE + place)

    def each(make, phase, piece, count, act):
        @pl.loop(1, count)
        def _(shift):
            getattr(make(phase, piece, shift), act)()

    for piece in range(own):
        each(plane_copy, 0, piece, PLANE, "start")
    for piece in range(own):
        part_in[piece, place] = part_ref[place * own + piece]
    loads[0].wait()
    loads[1].wait()
    for piece in range(own):
        each(plane_copy, 0, piece, PLANE, "wait_recv")
        part = part_in[piece].reshape(span, modes)
        spectrum = jnp.dot(high[...], part, preferred_element_type=jnp.float32) + jnp.dot(
            low[...], part, preferred_element_type=jnp.float32
        )
        spectrum = spectrum.reshape(sums.shape[1:])
        sums[piece] = spectrum
        partial_out[piece] = spectrum.astype(jnp.bfloat16)
        each(line_copy, 0, piece, outer, "start")
    for piece in range(own):
        each(line_copy, 0, piece, outer, "wait_recv")
        total = sums[piece, level]
        for shift in range(1, outer):
            total += partial_in[piece, shift].astype(jnp.float32)
        spec_out[:, piece] = total.reshape(PLANE, 2 * block_x, modes)
    each(plane_copy, 1, 0, PLANE, "start")
    spec_in[place] = spec_out[place]
    loads[2].wait()
    each(plane_copy, 1, 0, PLANE, "wait_recv")
    for mode in range(block_x):

        def add(at, carry, mode=mode):
            real, imag = carry
            for piece in range(own):
                a = spec_in[at, piece, mode : mode + 1, :]
                b = spec_in[at, piece, block_x + mode : block_x + mode + 1, :]
                c = weight[0, mode, at * own + piece].astype(jnp.float32)
                d = weight[1, mode, at * own + piece].astype(jnp.float32)
                real, imag = real + (a * c - b * d), imag + (a * d + b * c)
            return real, imag

        zero = jnp.zeros((channels, modes), jnp.float32)
        real, imag = lax.fori_loop(0, PLANE, add, (zero, zero))
        mix_out[:, :, mode, :] = real.reshape(PLANE, own, modes)
        mix_out[:, :, block_x + mode, :] = imag.reshape(PLANE, own, modes)
    each(plane_copy, 2, 0, PLANE, "start")
    mix_in[place] = mix_out[place]
    each(plane_copy, 2, 0, PLANE, "wait_recv")
    for piece in range(own):
        mixed = mix_in[:, piece].reshape(PLANE * 2 * block_x, modes)
        modes_in[piece, level] = mixed.astype(jnp.bfloat16)
        each(line_copy, 1, piece, outer, "start")
    loads[3].wait()
    for piece in range(own):
        each(line_copy, 1, piece, outer, "wait_recv")
        mixed = modes_in[piece].reshape(back.shape[1], modes)
        half = jnp.dot(back[...], mixed, preferred_element_type=jnp.float32)
        half_out[piece] = half.astype(jnp.bfloat16).reshape(half_out.shape[1:])
        each(plane_copy, 3, piece, PLANE, "start")
        out_ref[place * own + piece] = half_out[piece, place]
    for piece in range(own):
        each(plane_copy, 3, piece, PLANE, "wait_recv")
    for phase in range(4):
        for piece in range(own if phase in (0, 3) else 1):
            each(plane_copy, phase, piece, PLANE, "wait_send")
    for phase in range(2):
        for piece in range(own):
            each(line_copy, phase, piece, outer, "wait_send")


def remote_middle(partial_value, spec_weight, point_weight, bias, tables):
    outer = lax.axis_size("row") // PLANE
    channels, rows, modes = partial_value.shape
    block_x = spec_weight.shape[1]
    own = channels // PLANE
    span, depth = PLANE * rows, 2 * block_x
    size = CHUNK * channels
    vmem = pl.BlockSpec(memory_space=pltpu.VMEM)
    half, full = jnp.bfloat16, jnp.float32
    return pl.pallas_call(
        functools.partial(middle_kernel, outer),
        out_shape=[
            jax.ShapeDtypeStruct(partial_value.shape, half),
            jax.ShapeDtypeStruct((size, size), half),
            jax.ShapeDtypeStruct((size, size), full),
        ],
        in_specs=[vmem] * 3 + [pl.BlockSpec(memory_space=pl.ANY)] * 4,
        out_specs=[vmem] * 3,
        scratch_shapes=[
            pltpu.VMEM((outer * PLANE * depth, span), half),
            pltpu.VMEM((outer * PLANE * depth, span), half),
            pltpu.VMEM((span, outer * PLANE * depth), half),
            pltpu.VMEM(spec_weight.shape, half),
            pltpu.VMEM((own, PLANE, rows, modes), half),
            pltpu.VMEM((own, outer, PLANE * depth, modes), full),
            pltpu.VMEM((own, outer, PLANE * depth, modes), half),
            pltpu.VMEM((own, outer, PLANE * depth, modes), half),
            pltpu.VMEM((PLANE, own, depth, modes), full),
            pltpu.VMEM((PLANE, own, depth, modes), full),
            pltpu.VMEM((PLANE, own, depth, modes), full),
            pltpu.VMEM((PLANE, own, depth, modes), full),
            pltpu.VMEM((own, outer, PLANE * depth, modes), half),
            pltpu.VMEM((own, PLANE, rows, modes), half),
            pltpu.SemaphoreType.DMA((4,)),
            pltpu.SemaphoreType.DMA((6, own, PLANE)),
            pltpu.SemaphoreType.DMA((6, own, PLANE)),
        ],
        compiler_params=pltpu.CompilerParams(
            collective_id=0, has_side_effects=True, vmem_limit_bytes=32 * 1024 * 1024
        ),
    )(partial_value, point_weight, bias[None, :], *tables, spec_weight)


def shards(field, spec_weight, point_weight, bias):
    row_count, chan_count, col_count = field.shape
    row_devices = lax.axis_size("row")
    col_devices = lax.axis_size("col")
    block_x = spec_weight.shape[1]
    modes_y = spec_weight.shape[4] * col_devices
    modes_x = block_x * row_devices
    table_y, table_back = column_tables(modes_x, modes_y, col_count * col_devices)
    table_y, table_back = jnp.asarray(table_y), jnp.asarray(table_back)
    tables = [jnp.asarray(table) for table in row_tables(row_devices, block_x, row_count)]
    direct = col_devices == 1 and row_devices % PLANE == 0 and chan_count % PLANE == 0
    direct = direct and (2 * block_x) % 8 == 0 and row_count % 8 == 0
    if not direct:
        size = CHUNK * chan_count
        point = 0.5 * jnp.kron(jnp.eye(CHUNK, dtype=point_weight.dtype), point_weight)
        spread = 0.5 * jnp.broadcast_to(jnp.tile(bias, CHUNK)[:, None], (size, size))
    if col_devices > 1:
        start = lax.axis_index("col") * col_count
        table_y = lax.dynamic_slice_in_dim(table_y, start, col_count, 0)
        table_back = lax.dynamic_slice_in_dim(table_back, start, col_count, 1)
        whole = forward(field, table_y, jnp.float32)
        own = lax.psum_scatter(whole, "col", scatter_dimension=2, tiled=True)
        half = middle(own.astype(jnp.bfloat16), spec_weight, tables)
        half = lax.all_gather(half, "col", axis=2, tiled=True)
    else:
        partial_value = forward(field, table_y, jnp.bfloat16)
        if direct:
            half, point, spread = remote_middle(
                partial_value, spec_weight, point_weight, bias, tables
            )
        else:
            half = middle(partial_value, spec_weight, tables)
    half = half.reshape(chan_count, 2, row_count, modes_y).transpose(2, 0, 1, 3)
    half = half.reshape(row_count, chan_count, 2 * modes_y)
    return inverse(field, half, table_back, point, spread)


def solution(mesh):
    placed = (P(("group", "row"), None, "col"), P(None, "row", None, None, "col"), P(), P())
    return jax.shard_map(
        shards,
        mesh=mesh,
        in_specs=placed,
        out_specs=P(("group", "row"), None, "col"),
        check_vma=False,
    )
```

```python
import functools
import math

import jax
import jax.numpy as jnp
import ml_dtypes
import numpy as np
from jax import lax
from jax.experimental import pallas as pl
from jax.experimental.pallas import tpu as pltpu
from jax.sharding import PartitionSpec as P

BF16 = ml_dtypes.bfloat16
MESH = pl.DeviceIdType.MESH


def phases(first, second, length):
    index = (first[:, None].astype(np.int64) * second[None, :]) % length
    return index.astype(np.float32) * np.float32(2.0 * math.pi / length)


def column_tables(modes_x, modes_y, length_y):
    freq = np.arange(modes_y)
    phase = phases(np.arange(length_y), freq, length_y)
    cosine, sine = np.cos(phase), np.sin(phase)
    scale = np.float32(1.0 / math.sqrt(length_y))
    forward = np.concatenate([cosine * scale, -sine * scale], axis=1).astype(BF16)
    factor = np.where(freq == 0, 1.0, 2.0).astype(np.float32) / np.float32(
        math.sqrt(2.0 * modes_x * modes_y)
    )
    inverse = np.concatenate([factor * cosine, -factor * sine], axis=1).T.astype(BF16)
    halved = (0.5 * inverse.astype(np.float32)).astype(BF16)
    return forward, np.ascontiguousarray(halved)


def row_tables(row_devices, block_x, row_count):
    modes_x, length_x = row_devices * block_x, row_devices * row_count
    index = np.arange(modes_x)
    freq = np.where(index < modes_x // 2, index, index - modes_x + length_x)
    phase = phases(freq, np.arange(length_x), length_x)
    shape = (row_devices, 1, block_x, row_devices, row_count // CHUNK, 1, CHUNK)
    cosine, sine = np.cos(phase).reshape(shape), np.sin(phase).reshape(shape)
    table = np.concatenate(
        [np.concatenate([cosine, sine], axis=5), np.concatenate([-sine, cosine], axis=5)], axis=1
    ).reshape(2 * modes_x, 2 * length_x)
    scaled = table * np.float32(1.0 / math.sqrt(length_x))
    high = scaled.astype(BF16)
    low = (scaled - high.astype(np.float32)).astype(BF16)
    return high, low, np.ascontiguousarray(table.T).astype(BF16)


def regroup(rows, channels):
    out = np.zeros((rows * channels, rows * channels), BF16)
    for row in range(rows):
        for channel in range(channels):
            out[channel * rows + row, row * channels + channel] = 1
    return out


def regroup_back(rows, channels):
    out = np.zeros((2, rows * channels, channels * 2 * rows), BF16)
    for part in range(2):
        for row in range(rows):
            for channel in range(channels):
                out[part, row * channels + channel, (channel * 2 + part) * rows + row] = 1
    return out


CHUNK = 8


def forward_kernel(steps, field_ref, table_ref, perm_ref, out_ref, total, ordered):
    step = pl.program_id(0)
    rows, channels, width = field_ref.shape
    modes = out_ref.shape[2]

    @pl.when(step == 0)
    def _():
        total[...] = jnp.zeros_like(total)

    total[...] += jnp.dot(
        field_ref[...].reshape(rows * channels, width),
        table_ref[...],
        preferred_element_type=jnp.float32,
    )

    @pl.when(step == steps - 1)
    def _():
        size = CHUNK * channels
        for chunk in range(rows // CHUNK):
            part = total[chunk * size : (chunk + 1) * size, :]
            if out_ref.dtype == jnp.float32:
                moved = jnp.dot(
                    perm_ref[...].astype(jnp.float32),
                    part,
                    preferred_element_type=jnp.float32,
                    precision=lax.Precision.HIGHEST,
                )
            else:
                moved = jnp.dot(
                    perm_ref[...], part.astype(jnp.bfloat16), preferred_element_type=jnp.float32
                )
            moved = moved.reshape(channels, CHUNK, 2 * modes)
            at = 2 * chunk * CHUNK
            ordered[:, at : at + CHUNK, :] = moved[:, :, :modes]
            ordered[:, at + CHUNK : at + 2 * CHUNK, :] = moved[:, :, modes:]
        out_ref[...] = ordered[...].astype(out_ref.dtype)


def forward(field, table, out_type):
    rows, channels, cols = field.shape
    modes = table.shape[1] // 2
    width = min(cols, 2048)
    steps = cols // width
    perm = regroup(CHUNK, channels)
    return pl.pallas_call(
        functools.partial(forward_kernel, steps),
        out_shape=jax.ShapeDtypeStruct((channels, 2 * rows, modes), out_type),
        grid=(steps,),
        in_specs=[
            pl.BlockSpec((rows, channels, width), lambda y: (0, 0, y)),
            pl.BlockSpec((width, 2 * modes), lambda y: (y, 0)),
            pl.BlockSpec(perm.shape, lambda y: (0, 0)),
        ],
        out_specs=pl.BlockSpec((channels, 2 * rows, modes), lambda y: (0, 0, 0)),
        scratch_shapes=[
            pltpu.VMEM((rows * channels, 2 * modes), jnp.float32),
            pltpu.VMEM((channels, 2 * rows, modes), jnp.float32),
        ],
        compiler_params=pltpu.CompilerParams(vmem_limit_bytes=60 * 1024 * 1024),
        cost_estimate=pl.CostEstimate(
            flops=2 * rows * channels * cols * 2 * modes,
            bytes_accessed=2 * (rows * channels * cols + cols * 2 * modes),
            transcendentals=0,
        ),
    )(field, table, jnp.asarray(perm))


def inverse_kernel(
    field_ref, half_ref, perm_ref, table_ref, point_ref, bias_ref, out_ref, ordered
):
    rows, channels, width = field_ref.shape
    size = CHUNK * channels
    tile = min(width, 256)
    modes = half_ref.shape[2]

    @pl.when(pl.program_id(0) == 0)
    def _():
        for chunk in range(rows // CHUNK):
            at = 2 * CHUNK * chunk
            part = half_ref[:, at : at + 2 * CHUNK, :].reshape(2 * size, modes)
            for side in range(2):
                moved = jnp.dot(perm_ref[side], part, preferred_element_type=jnp.float32)
                ordered[chunk, :, side * modes : (side + 1) * modes] = moved.astype(jnp.bfloat16)

    @pl.loop(0, rows // CHUNK)
    def _(chunk):
        at = pl.multiple_of(chunk * CHUNK, CHUNK)
        half = ordered[chunk]
        for col in range(0, width, tile):
            values = field_ref[pl.ds(at, CHUNK), :, col : col + tile].reshape(size, tile)
            x = (
                jnp.dot(half, table_ref[:, col : col + tile], preferred_element_type=jnp.float32)
                + jnp.dot(point_ref[...], values, preferred_element_type=jnp.float32)
                + bias_ref[:, :tile]
            )
            rate = 2.0 * math.sqrt(2.0 / math.pi)
            y = x * jnp.tanh(x * (rate * 4.0 * 0.044715 * (x * x) + rate)) + x
            out_ref[pl.ds(at, CHUNK), :, col : col + tile] = y.astype(out_ref.dtype).reshape(
                CHUNK, channels, tile
            )


def inverse(field, half, table, point, spread):
    rows, channels, cols = field.shape
    depth = table.shape[0]
    width = min(cols, 2048)
    size = CHUNK * channels
    perm = regroup_back(CHUNK, channels)
    return pl.pallas_call(
        inverse_kernel,
        out_shape=jax.ShapeDtypeStruct(field.shape, jnp.bfloat16),
        grid=(cols // width,),
        in_specs=[
            pl.BlockSpec((rows, channels, width), lambda y: (0, 0, y)),
            pl.BlockSpec(half.shape, lambda y: (0, 0, 0)),
            pl.BlockSpec(perm.shape, lambda y: (0, 0, 0)),
            pl.BlockSpec((depth, width), lambda y: (0, y)),
            pl.BlockSpec(point.shape, lambda y: (0, 0)),
            pl.BlockSpec(spread.shape, lambda y: (0, 0)),
        ],
        out_specs=pl.BlockSpec((rows, channels, width), lambda y: (0, 0, y)),
        scratch_shapes=[pltpu.VMEM((rows // CHUNK, size, depth), jnp.bfloat16)],
        compiler_params=pltpu.CompilerParams(vmem_limit_bytes=60 * 1024 * 1024),
        cost_estimate=pl.CostEstimate(
            flops=2 * rows * channels * cols * (depth + size),
            bytes_accessed=4 * rows * channels * cols,
            transcendentals=rows * channels * cols,
        ),
    )(field, half, jnp.asarray(perm), table, point, spread)


def mix_modes(spectrum, spec_weight):
    weights = spec_weight.astype(jnp.float32)
    real, imag = spectrum[:, 0], spectrum[:, 1]
    product = functools.partial(jnp.einsum, "ijk,jiok->ojk", precision=lax.Precision.HIGHEST)
    out_real = product(real, weights[0]) - product(imag, weights[1])
    out_imag = product(real, weights[1]) + product(imag, weights[0])
    return jnp.stack([out_real, out_imag], axis=1).astype(jnp.bfloat16)


def swap(blocks):
    count, own, rows, modes = blocks.shape
    got = lax.all_to_all(blocks, "row", 0, 0, tiled=True)
    return got.transpose(1, 0, 2, 3).reshape(own, count * rows, modes)


def give(values, count):
    own, size, modes = values.shape
    blocks = values.reshape(own, count, size // count, modes).transpose(1, 0, 2, 3)
    got = lax.all_to_all(blocks, "row", 0, 0, tiled=True)
    return got.reshape(count * own, size // count, modes)


def middle(partial_value, spec_weight, tables):
    high, low, back = tables
    channels, rows, modes = partial_value.shape
    count = lax.axis_size("row")
    block_x = spec_weight.shape[1]
    part = swap(partial_value.reshape(count, channels // count, rows, modes))
    transform = functools.partial(
        jnp.einsum, "am,cmk->cak", preferred_element_type=jnp.float32
    )
    spectrum = give(transform(high, part) + transform(low, part), count)
    mixed = mix_modes(spectrum.reshape(channels, 2, block_x, modes), spec_weight)
    mixed = swap(mixed.reshape(count, channels // count, 2 * block_x, modes))
    half = jnp.einsum("ma,cak->cmk", back, mixed, preferred_element_type=jnp.float32)
    return give(half.astype(jnp.bfloat16), count)


PLANE = 8


def middle_kernel(
    outer, perm_ref, point_ref, bias_ref, field_hbm, table_hbm, high_hbm, low_hbm, back_hbm,
    weight_hbm, out_ref, point_out, bias_out,
    field, table, part_out, high, low, back, weight, part_in, sums, partial_out, partial_in, spec_out, spec_in,
    mix_out, mix_in, modes_in, half_out, field_sem, table_sem, load_sem, send_sem, recv_sem,
):
    me = lax.axis_index("row")
    level, place = me // PLANE, lax.rem(me, PLANE)
    block_x, channels, modes = weight.shape[1], weight.shape[3], weight.shape[4]
    own = channels // PLANE
    span = high.shape[1]
    start = pl.multiple_of(level * span, span)
    pairs = [
        (high_hbm.at[:, pl.ds(start, span)], high),
        (low_hbm.at[:, pl.ds(start, span)], low),
        (weight_hbm, weight),
        (back_hbm.at[pl.ds(start, span), :], back),
    ]
    loads = [
        pltpu.make_async_copy(src, dst, load_sem.at[at]) for at, (src, dst) in enumerate(pairs)
    ]
    chunks, slices, size = field.shape[0], field.shape[1], CHUNK * channels
    width = field.shape[4]

    def load_field(chunk, at):
        rows = pl.ds(pl.multiple_of(chunk * CHUNK, CHUNK), CHUNK)
        return pltpu.make_async_copy(
            field_hbm.at[rows, :, at * width : (at + 1) * width],
            field.at[chunk, at],
            field_sem.at[chunk, at],
        )

    def load_table(at):
        return pltpu.make_async_copy(
            table_hbm.at[at * width : (at + 1) * width, :], table.at[at], table_sem.at[at]
        )

    for at in range(slices):
        load_table(at).start()
        load_field(0, at).start()

    def in_plane(shift):
        return lax.rem(place + shift, PLANE)

    def in_line(shift):
        return lax.rem(level + shift, outer)

    barrier = pltpu.get_barrier_semaphore()

    @pl.loop(1, PLANE)
    def _(shift):
        to = level * PLANE + in_plane(shift)
        pl.semaphore_signal(barrier, inc=1, device_id={"row": to}, device_id_type=MESH)

    @pl.loop(1, outer)
    def _(shift):
        to = in_line(shift) * PLANE + place
        pl.semaphore_signal(barrier, inc=1, device_id={"row": to}, device_id_type=MESH)

    shape = (size, channels)
    pick = lax.broadcasted_iota(jnp.int32, shape, 0) % channels == lax.broadcasted_iota(
        jnp.int32, shape, 1
    )
    pick = pick.astype(jnp.float32)
    along = (((1,), (1,)), ((), ()))
    tall = jnp.dot(pick.astype(jnp.bfloat16), point_ref[...], preferred_element_type=jnp.float32)
    full = lax.dot_general(
        tall.astype(jnp.bfloat16),
        pick.astype(jnp.bfloat16),
        along,
        preferred_element_type=jnp.float32,
    )
    shape = (size, size)
    same = lax.broadcasted_iota(jnp.int32, shape, 0) // channels == lax.broadcasted_iota(
        jnp.int32, shape, 1
    ) // channels
    point_out[...] = jnp.where(same, 0.5 * full, 0.0).astype(jnp.bfloat16)
    bias_out[...] = 0.5 * lax.dot_general(
        pick,
        jnp.broadcast_to(bias_ref[...], (size, channels)),
        along,
        preferred_element_type=jnp.float32,
        precision=lax.Precision.HIGHEST,
    )
    pl.semaphore_wait(barrier, PLANE - 1 + outer - 1)

    def copy(src, dst, phase, piece, shift, to):
        return pltpu.make_async_remote_copy(
            src_ref=src,
            dst_ref=dst,
            send_sem=send_sem.at[phase, piece, shift],
            recv_sem=recv_sem.at[phase, piece, shift],
            device_id={"row": to},
            device_id_type=MESH,
        )

    def plane_copy(phase, piece, shift):
        to = in_plane(shift)
        src, dst = [
            lambda: (part_out.at[piece, pl.ds(to * own, own)], part_in.at[place, piece]),
            lambda: (spec_out.at[to], spec_in.at[place]),
            lambda: (mix_out.at[to], mix_in.at[place]),
            lambda: (half_out.at[piece, to], out_ref.at[place * own + piece]),
        ][phase]()
        return copy(src, dst, phase, piece, shift, level * PLANE + to)

    def line_copy(phase, piece, shift):
        to = in_line(shift)
        src, dst = [
            lambda: (partial_out.at[piece, to], partial_in.at[piece, shift]),
            lambda: (modes_in.at[piece, level], modes_in.at[piece, level]),
        ][phase]()
        return copy(src, dst, 4 + phase, piece, shift, to * PLANE + place)

    def each(make, phase, piece, count, act):
        @pl.loop(1, count)
        def _(shift):
            getattr(make(phase, piece, shift), act)()

    @pl.loop(0, chunks)
    def _(chunk):
        @pl.when(chunk < chunks - 1)
        def _():
            for at in range(slices):
                load_field(chunk + 1, at).start()

        @pl.when(chunk == chunks - 1)
        def _():
            for load in loads:
                load.start()

        total = jnp.zeros((size, 2 * modes), jnp.float32)
        for at in range(slices):

            @pl.when(chunk == 0)
            def _():
                load_table(at).wait()

            load_field(chunk, at).wait()
            total += jnp.dot(
                field[chunk, at].reshape(size, width),
                table[at],
                preferred_element_type=jnp.float32,
            )
        moved = jnp.dot(
            perm_ref[...], total.astype(jnp.bfloat16), preferred_element_type=jnp.float32
        )
        moved = moved.reshape(channels, CHUNK, 2 * modes)
        moved = jnp.stack([moved[:, :, :modes], moved[:, :, modes:]], axis=1)
        moved = moved.reshape(channels, 2 * CHUNK, modes).astype(jnp.bfloat16)
        part_out[chunk] = moved
        each(plane_copy, 0, chunk, PLANE, "start")
        part_in[place, chunk] = part_out[chunk, pl.ds(place * own, own)]

    loads[0].wait()
    loads[1].wait()

    @pl.loop(0, chunks)
    def _(chunk):
        each(plane_copy, 0, chunk, PLANE, "wait_recv")

    for piece in range(own):
        part = part_in[:, :, piece].reshape(span, modes)
        spectrum = jnp.dot(high[...], part, preferred_element_type=jnp.float32) + jnp.dot(
            low[...], part, preferred_element_type=jnp.float32
        )
        spectrum = spectrum.reshape(sums.shape[1:])
        sums[piece] = spectrum
        partial_out[piece] = spectrum.astype(jnp.bfloat16)
        each(line_copy, 0, piece, outer, "start")
    for piece in range(own):
        each(line_copy, 0, piece, outer, "wait_recv")
        total = sums[piece, level]
        for shift in range(1, outer):
            total += partial_in[piece, shift].astype(jnp.float32)
        spec_out[:, piece] = total.reshape(PLANE, 2 * block_x, modes)
    each(plane_copy, 1, 0, PLANE, "start")
    spec_in[place] = spec_out[place]
    loads[2].wait()
    each(plane_copy, 1, 0, PLANE, "wait_recv")
    for mode in range(block_x):

        def add(at, carry, mode=mode):
            real, imag = carry
            for piece in range(own):
                a = spec_in[at, piece, mode : mode + 1, :]
                b = spec_in[at, piece, block_x + mode : block_x + mode + 1, :]
                c = weight[0, mode, at * own + piece].astype(jnp.float32)
                d = weight[1, mode, at * own + piece].astype(jnp.float32)
                real, imag = real + (a * c - b * d), imag + (a * d + b * c)
            return real, imag

        zero = jnp.zeros((channels, modes), jnp.float32)
        real, imag = lax.fori_loop(0, PLANE, add, (zero, zero))
        mix_out[:, :, mode, :] = real.reshape(PLANE, own, modes)
        mix_out[:, :, block_x + mode, :] = imag.reshape(PLANE, own, modes)
    each(plane_copy, 2, 0, PLANE, "start")
    mix_in[place] = mix_out[place]
    each(plane_copy, 2, 0, PLANE, "wait_recv")
    for piece in range(own):
        mixed = mix_in[:, piece].reshape(PLANE * 2 * block_x, modes)
        modes_in[piece, level] = mixed.astype(jnp.bfloat16)
        each(line_copy, 1, piece, outer, "start")
    loads[3].wait()
    for piece in range(own):
        each(line_copy, 1, piece, outer, "wait_recv")
        mixed = modes_in[piece].reshape(back.shape[1], modes)
        half = jnp.dot(back[...], mixed, preferred_element_type=jnp.float32)
        half_out[piece] = half.astype(jnp.bfloat16).reshape(half_out.shape[1:])
        each(plane_copy, 3, piece, PLANE, "start")
        out_ref[place * own + piece] = half_out[piece, place]
    for piece in range(own):
        each(plane_copy, 3, piece, PLANE, "wait_recv")
    for phase, count in enumerate((chunks, 1, 1, own)):
        for piece in range(count):
            each(plane_copy, phase, piece, PLANE, "wait_send")
    for phase in range(2):
        for piece in range(own):
            each(line_copy, phase, piece, outer, "wait_send")


def remote_middle(field, table, spec_weight, point_weight, bias, tables):
    outer = lax.axis_size("row") // PLANE
    channels, rows, modes = field.shape[1], 2 * field.shape[0], spec_weight.shape[4]
    chunks = field.shape[0] // CHUNK
    width = min(field.shape[2], 2048)
    slices = field.shape[2] // width
    perm = regroup(CHUNK, channels)
    block_x = spec_weight.shape[1]
    own = channels // PLANE
    span, depth = PLANE * rows, 2 * block_x
    size = CHUNK * channels
    vmem = pl.BlockSpec(memory_space=pltpu.VMEM)
    half, full = jnp.bfloat16, jnp.float32
    return pl.pallas_call(
        functools.partial(middle_kernel, outer),
        out_shape=[
            jax.ShapeDtypeStruct((channels, rows, modes), half),
            jax.ShapeDtypeStruct((size, size), half),
            jax.ShapeDtypeStruct((size, size), full),
        ],
        in_specs=[vmem] * 3 + [pl.BlockSpec(memory_space=pl.ANY)] * 6,
        out_specs=[vmem] * 3,
        scratch_shapes=[
            pltpu.VMEM((chunks, slices, CHUNK, channels, width), half),
            pltpu.VMEM((slices, width, 2 * modes), half),
            pltpu.VMEM((chunks, channels, 2 * CHUNK, modes), half),
            pltpu.VMEM((outer * PLANE * depth, span), half),
            pltpu.VMEM((outer * PLANE * depth, span), half),
            pltpu.VMEM((span, outer * PLANE * depth), half),
            pltpu.VMEM(spec_weight.shape, half),
            pltpu.VMEM((PLANE, chunks, own, 2 * CHUNK, modes), half),
            pltpu.VMEM((own, outer, PLANE * depth, modes), full),
            pltpu.VMEM((own, outer, PLANE * depth, modes), half),
            pltpu.VMEM((own, outer, PLANE * depth, modes), half),
            pltpu.VMEM((PLANE, own, depth, modes), full),
            pltpu.VMEM((PLANE, own, depth, modes), full),
            pltpu.VMEM((PLANE, own, depth, modes), full),
            pltpu.VMEM((PLANE, own, depth, modes), full),
            pltpu.VMEM((own, outer, PLANE * depth, modes), half),
            pltpu.VMEM((own, PLANE, rows, modes), half),
            pltpu.SemaphoreType.DMA((chunks, slices)),
            pltpu.SemaphoreType.DMA((slices,)),
            pltpu.SemaphoreType.DMA((4,)),
            pltpu.SemaphoreType.DMA((6, max(own, chunks), PLANE)),
            pltpu.SemaphoreType.DMA((6, max(own, chunks), PLANE)),
        ],
        compiler_params=pltpu.CompilerParams(
            collective_id=0, has_side_effects=True, vmem_limit_bytes=60 * 1024 * 1024
        ),
    )(jnp.asarray(perm), point_weight, bias[None, :], field, table, *tables, spec_weight)


def shards(field, spec_weight, point_weight, bias):
    row_count, chan_count, col_count = field.shape
    row_devices = lax.axis_size("row")
    col_devices = lax.axis_size("col")
    block_x = spec_weight.shape[1]
    modes_y = spec_weight.shape[4] * col_devices
    modes_x = block_x * row_devices
    table_y, table_back = column_tables(modes_x, modes_y, col_count * col_devices)
    table_y, table_back = jnp.asarray(table_y), jnp.asarray(table_back)
    tables = [jnp.asarray(table) for table in row_tables(row_devices, block_x, row_count)]
    direct = col_devices == 1 and row_devices % PLANE == 0 and chan_count % PLANE == 0
    direct = direct and (2 * block_x) % 8 == 0 and row_count % 8 == 0
    if not direct:
        size = CHUNK * chan_count
        point = 0.5 * jnp.kron(jnp.eye(CHUNK, dtype=point_weight.dtype), point_weight)
        spread = 0.5 * jnp.broadcast_to(jnp.tile(bias, CHUNK)[:, None], (size, size))
    if col_devices > 1:
        start = lax.axis_index("col") * col_count
        table_y = lax.dynamic_slice_in_dim(table_y, start, col_count, 0)
        table_back = lax.dynamic_slice_in_dim(table_back, start, col_count, 1)
        whole = forward(field, table_y, jnp.float32)
        own = lax.psum_scatter(whole, "col", scatter_dimension=2, tiled=True)
        half = middle(own.astype(jnp.bfloat16), spec_weight, tables)
        half = lax.all_gather(half, "col", axis=2, tiled=True)
    elif direct:
        half, point, spread = remote_middle(
            field, table_y, spec_weight, point_weight, bias, tables
        )
    else:
        half = middle(forward(field, table_y, jnp.bfloat16), spec_weight, tables)
    return inverse(field, half, table_back, point, spread)


def solution(mesh):
    placed = (P(("group", "row"), None, "col"), P(None, "row", None, None, "col"), P(), P())
    return jax.shard_map(
        shards,
        mesh=mesh,
        in_specs=placed,
        out_specs=P(("group", "row"), None, "col"),
        check_vma=False,
    )
```
